512 devices in a mesh: leaf: 8 (over x, core), col: 64 (over z, y).
Axes of the slice: x: 4, y: 8, z: 8, core: 2. Of those that a mesh axis runs over, the one named last changes fastest.
Arguments:
- child_panels: bfloat16 [8, 8192, 2048], P('leaf', 'col'), may hold values from -6 to 6
- child_links: bfloat16 [8, 512, 2048], P('leaf', 'col'), may hold values from -6 to 6
- child_pivots: bfloat16 [8, 1024, 1024], P('leaf', 'col'), may hold values from -6 to 6
- child_inverse: bfloat16 [8, 2, 1024, 1024], P('leaf', None, 'col'), as said below
- block_mask: int32 [8, 64, 2], P('leaf', 'col'), may hold values from 0 to 1, as said below
- row_map: int32 [8, 8192], P('leaf', 'col'), may hold values from 0 to 255, as said below
- parent_panels: bfloat16 [8, 8192, 2048], P('leaf', 'col'), may hold values from -6 to 6
- parent_pivots: bfloat16 [4, 1024, 1024], P(None, 'col'), may hold values from -6 to 6
- parent_inverse: bfloat16 [4, 2, 1024, 1024], P(None, None, 'col'), as said below
Outputs:
- child_factor: bfloat16 [8, 8192, 2048], P('leaf', 'col')
- parent_factor: bfloat16 [8, 8192, 2048], P('leaf', 'col')
The draws below stay inside these ranges and needn't reach their ends.
Inputs may be any that keep to these rules, and one draw needn't show every extreme that they name: block_mask[f, b, 1] >= block_mask[f, b, 0]: a row block present in a front's first panel is present in its second. `row_map`: within each block of 128 consecutive rows of one front the values are distinct. Each child_inverse[f, k] is lower triangular. Each parent_inverse[p, k] is lower triangular.
All inputs are finite; a program needn't handle non-finite values.
Results may differ from the reference program's by a relative error of at most 0.011.
Values may be sent and summed in bfloat16 or wider, within the bound.
No kernel may reach another device: no remote copies, remote signals or barrier semaphores. Data moves between devices by JAX's collectives and lax.ppermute only.
A program may use at most 64 MiB of HBM per device.

```python
import jax
import jax.numpy as jnp
from jax import lax

PANEL = 1024
LINK = 512
ROWS_DEV = 128
FRONTS = 8
PARENTS = 4
CROWS = 8192


def assemble_factor(spread, diagonal_part):
    row_index = lax.broadcasted_iota(jnp.int32, spread.shape, spread.ndim - 2)
    column = lax.broadcasted_iota(jnp.int32, spread.shape, spread.ndim - 1)
    entries = jnp.where(row_index > column, spread * PANEL ** (-0.5), jnp.where(row_index == column, diagonal_part, 0.0))
    return entries * PANEL ** (-0.25)


def draw_child_inverse(key, part):
    key = jax.random.fold_in(key, 11)
    full_shape = (FRONTS, 2, PANEL, PANEL)
    first_key, second_key = jax.random.split(key)
    spread = jax.random.normal(first_key, full_shape, jnp.float32)
    diagonal_part = jnp.exp(jax.random.uniform(second_key, full_shape, jnp.float32, -0.6931472, 0.6931472))
    return assemble_factor(spread, diagonal_part).astype(jnp.bfloat16)


def draw_parent_inverse(key, part):
    key = jax.random.fold_in(key, 12)
    full_shape = (PARENTS, 2, PANEL, PANEL)
    first_key, second_key = jax.random.split(key)
    spread = jax.random.normal(first_key, full_shape, jnp.float32)
    diagonal_part = jnp.exp(jax.random.uniform(second_key, full_shape, jnp.float32, -0.6931472, 0.6931472))
    return assemble_factor(spread, diagonal_part).astype(jnp.bfloat16)


def draw_block_mask(key, part):
    key = jax.random.fold_in(key, 13)
    first_key, second_key = jax.random.split(key)
    blocks = CROWS // 128
    block_index = lax.broadcasted_iota(jnp.int32, (FRONTS, blocks), 1)
    threshold = 16 + 48 * block_index // blocks
    first_panel = (jax.random.randint(first_key, (FRONTS, blocks), 0, 64) < threshold).astype(jnp.int32)
    second_panel = jnp.maximum(first_panel, jax.random.randint(second_key, (FRONTS, blocks), 0, 2))
    return jnp.stack([first_panel, second_panel], -1).astype(jnp.int32)


def draw_row_map(key, part):
    key = jax.random.fold_in(key, 14)
    block_keys = jax.random.split(key, FRONTS * (CROWS // ROWS_DEV))
    chosen = jax.vmap(lambda block_key: jax.random.permutation(block_key, 2 * ROWS_DEV)[:ROWS_DEV])(block_keys)
    return chosen.reshape(FRONTS, CROWS).astype(jnp.int32)


def shard_levels(rng, shape, shards, smallest, high):
    gain, own = 1.0, jax.random.fold_in(rng, 6)
    for axis_at, blocks in shards:
        steps = jnp.exp(jax.random.uniform(jax.random.fold_in(own, axis_at), (blocks,), jnp.float32, smallest / len(shards), high / len(shards)))
        gain = gain * jnp.repeat(steps, shape[axis_at] // blocks).reshape([-1 if axis == axis_at else 1 for axis in range(len(shape))])
    return gain


def scatter_about(rng, shape, deviation, limit, cuts=(), held_as=jnp.bfloat16):
    array = deviation * jax.random.normal(rng, shape, jnp.float32)
    if cuts:
        array = array * shard_levels(rng, shape, cuts, -0.22, 0.18)
    return jnp.clip(array, -limit, limit).astype(held_as)


def setup_inputs(seed: int = 0) -> dict:
    keys = jax.random.split(jax.random.key(seed), 10)
    child_panels = scatter_about(keys[0], (FRONTS, CROWS, 2 * PANEL), 1.0, 6.0, ((0, 8), (1, 64)))
    child_links = scatter_about(keys[1], (FRONTS, LINK, 2 * PANEL), 1.0, 6.0, ((0, 8), (1, 64)))
    child_pivots = scatter_about(keys[2], (FRONTS, PANEL, PANEL), 1.0, 6.0, ((0, 8), (1, 64)))
    child_inverse = draw_child_inverse(jax.random.fold_in(keys[9], 71), 0)
    block_mask = draw_block_mask(jax.random.fold_in(keys[9], 71), 0)
    row_map = draw_row_map(jax.random.fold_in(keys[9], 71), 0)
    parent_panels = scatter_about(keys[6], (FRONTS, CROWS, 2 * PANEL), 1.0, 6.0, ((0, 8), (1, 64)))
    parent_pivots = scatter_about(keys[7], (PARENTS, PANEL, PANEL), 1.0, 6.0, ((1, 64),))
    parent_inverse = draw_parent_inverse(jax.random.fold_in(keys[9], 71), 0)
    return dict(child_panels=child_panels, child_links=child_links, child_pivots=child_pivots, child_inverse=child_inverse, block_mask=block_mask, row_map=row_map, parent_panels=parent_panels, parent_pivots=parent_pivots, parent_inverse=parent_inverse)


def transposed_product(left, right):
    return jnp.dot(left, right.T, preferred_element_type=jnp.float32)


def reference(child_panels, child_links, child_pivots, child_inverse, block_mask, row_map, parent_panels, parent_pivots, parent_inverse):
    width = PANEL
    child_out = []
    spread_parts = []
    for front_index in range(FRONTS):
        keep_rows = jnp.repeat(block_mask[front_index], 128, axis=0).astype(jnp.bfloat16)
        first_input = child_panels[front_index, :, :width] * keep_rows[:, 0:1]
        second_input = child_panels[front_index, :, width:] * keep_rows[:, 1:2]
        link_rows = child_links[front_index]
        stacked = jnp.concatenate([first_input, link_rows[:, :width], child_pivots[front_index]], 0)
        first_all = transposed_product(stacked, child_inverse[front_index, 0]).astype(jnp.bfloat16)
        child_first = first_all[:CROWS]
        link_first = first_all[CROWS:CROWS + LINK]
        pivot_first = first_all[CROWS + LINK:]
        upper_rows = jnp.concatenate([child_first, link_first], 0)
        second_rhs = (jnp.concatenate([second_input, link_rows[:, width:]], 0).astype(jnp.float32) - transposed_product(upper_rows, pivot_first)).astype(jnp.bfloat16)
        second_all = transposed_product(second_rhs, child_inverse[front_index, 1]).astype(jnp.bfloat16)
        factor = jnp.concatenate([child_first, second_all[:CROWS]], 1)
        link_factor = jnp.concatenate([link_first, second_all[CROWS:]], 1)
        contribution = -transposed_product(factor, link_factor)
        block_index = (jnp.arange(CROWS) // ROWS_DEV).astype(jnp.int32)
        target_rows = row_map[front_index].astype(jnp.int32)
        dest_front = (target_rows // ROWS_DEV).astype(jnp.int32)
        dest_row = (block_index * ROWS_DEV + target_rows % ROWS_DEV).astype(jnp.int32)
        placed = jnp.zeros((2, CROWS, LINK), jnp.float32).at[dest_front, dest_row].add(contribution)
        spread_parts.append(placed)
        child_out.append(factor)
    parent_out = []
    for parent_index in range(PARENTS):
        even_part = spread_parts[2 * parent_index]
        odd_part = spread_parts[2 * parent_index + 1]
        inputs = []
        for half_index in range(2):
            extension = jnp.concatenate([even_part[half_index], odd_part[half_index]], 1)
            panel_part = parent_panels[2 * parent_index + half_index, :, :width].astype(jnp.float32)
            inputs.append((panel_part + extension).astype(jnp.bfloat16))
        stacked = jnp.concatenate(inputs + [parent_pivots[parent_index]], 0)
        first_all = transposed_product(stacked, parent_inverse[parent_index, 0]).astype(jnp.bfloat16)
        parent_first = first_all[:2 * CROWS]
        pivot_first = first_all[2 * CROWS:]
        second_panel = jnp.concatenate([parent_panels[2 * parent_index, :, width:], parent_panels[2 * parent_index + 1, :, width:]], 0)
        parent_rhs = (second_panel.astype(jnp.float32) - transposed_product(parent_first, pivot_first)).astype(jnp.bfloat16)
        parent_second = transposed_product(parent_rhs, parent_inverse[parent_index, 1]).astype(jnp.bfloat16)
        joined = jnp.concatenate([parent_first, parent_second], 1)
        parent_out.append(joined[:CROWS])
        parent_out.append(joined[CROWS:])
    return jnp.stack(child_out, 0), jnp.stack(parent_out, 0)
```

```python
import jax
import jax.numpy as jnp
from jax import lax
from jax.sharding import PartitionSpec as P


def partner(value, axis, stride):
    return lax.ppermute(value, axis, [(i, i ^ 1 << stride) for i in range(lax.axis_size(axis))])


def times_rows(left_rows, segment):
    return lax.dot_general(
        left_rows, segment, (((1,), (1,)), ((), ())), preferred_element_type=jnp.float32
    )


def local(
    child_panels,
    child_links,
    child_pivots,
    child_inverse,
    block_mask,
    row_map,
    parent_panels,
    parent_pivots,
    parent_inverse,
):
    bf16 = jnp.bfloat16
    width = child_pivots.shape[2]
    rows = child_panels.shape[1]
    shard = child_pivots.shape[1]
    link_shard = child_links.shape[1]
    leaf = lax.axis_index("leaf")
    sibling_bit = leaf % 2
    parent_index = leaf // 2

    half = shard // 2
    mine_inverse = lax.dynamic_slice(
        parent_inverse, (parent_index, sibling_bit, 0, 0), (1, 1, shard, width)
    )[0, 0]
    mine_pivots = lax.dynamic_slice(
        parent_pivots, (parent_index, sibling_bit * half, 0), (1, half, width)
    )[0]
    packed = jnp.concatenate(
        [
            child_inverse[0, 0],
            child_pivots[0],
            child_links[0, :, :width],
            child_links[0, :, width:],
            child_inverse[0, 1],
            mine_inverse,
            mine_pivots,
        ],
        0,
    )
    gathered = lax.all_gather(packed, "col", axis=0, tiled=False)

    def part(start, count):
        return gathered[:, start : start + count].reshape(-1, width)

    inverse_0 = part(0, shard)
    pivots = part(shard, shard)
    links_0 = part(2 * shard, link_shard)
    links_1 = part(2 * shard + link_shard, link_shard)
    inverse_1 = part(2 * shard + 2 * link_shard, shard)
    at = 3 * shard + 2 * link_shard
    mine = gathered[:, at:]
    theirs = partner(mine, "leaf", 0)

    flags = block_mask[0, 0].astype(bf16)
    first_input = child_panels[0, :, :width] * flags[0]
    second_input = child_panels[0, :, width:] * flags[1]
    link_count = links_0.shape[0]
    first_all = times_rows(
        jnp.concatenate([first_input, links_0, pivots], 0), inverse_0
    ).astype(bf16)
    child_first = first_all[:rows]
    pivot_first = first_all[rows + link_count :]
    update = times_rows(first_all[: rows + link_count], pivot_first)
    second_source = jnp.concatenate([second_input, links_1], 0)
    second_rhs = (second_source.astype(jnp.float32) - update).astype(bf16)
    second_all = times_rows(second_rhs, inverse_1).astype(bf16)
    child_second = second_all[:rows]
    child_factor = jnp.concatenate([child_first, child_second], 1)
    contribution = -(
        times_rows(child_first, first_all[rows : rows + link_count])
        + times_rows(child_second, second_all[rows:])
    )
    placed = (
        jnp.zeros((2 * rows, contribution.shape[1]), jnp.float32)
        .at[row_map[0]]
        .add(contribution)
    )
    own_part = lax.dynamic_slice_in_dim(placed, sibling_bit * rows, rows, 0)
    sent_part = lax.dynamic_slice_in_dim(placed, (1 - sibling_bit) * rows, rows, 0)
    received = partner(sent_part, "leaf", 0)
    even = sibling_bit == 0
    extension = jnp.where(
        even,
        jnp.concatenate([own_part, received], 1),
        jnp.concatenate([received, own_part], 1),
    )
    parent_input = (parent_panels[0, :, :width].astype(jnp.float32) + extension).astype(bf16)

    low = jnp.where(even, mine, theirs)
    high = jnp.where(even, theirs, mine)
    parent_inverse_0 = low[:, :shard].reshape(-1, width)
    parent_inverse_1 = high[:, :shard].reshape(-1, width)
    parent_pivot_rows = jnp.concatenate([low[:, shard:], high[:, shard:]], 1).reshape(-1, width)
    parent_pivot_first = times_rows(parent_pivot_rows, parent_inverse_0).astype(bf16)
    parent_first = times_rows(parent_input, parent_inverse_0).astype(bf16)
    parent_update = times_rows(parent_first, parent_pivot_first)
    parent_rhs = (parent_panels[0, :, width:].astype(jnp.float32) - parent_update).astype(bf16)
    parent_second = times_rows(parent_rhs, parent_inverse_1).astype(bf16)
    parent_factor = jnp.concatenate([parent_first, parent_second], 1)
    return (child_factor[None], parent_factor[None])


def solution(mesh):
    return jax.shard_map(
        local,
        mesh=mesh,
        in_specs=(
            P("leaf", "col", None),
            P("leaf", "col", None),
            P("leaf", "col", None),
            P("leaf", None, "col", None),
            P("leaf", "col", None),
            P("leaf", "col"),
            P("leaf", "col", None),
            P(None, "col", None),
            P(None, None, "col", None),
        ),
        out_specs=(P("leaf", "col", None), P("leaf", "col", None)),
        check_vma=False,
    )
```

```python
import functools

import jax
import jax.numpy as jnp
from jax import lax
from jax.experimental import pallas as pl
from jax.experimental.pallas import tpu as pltpu
from jax.sharding import PartitionSpec as P

BF16, F32 = jnp.bfloat16, jnp.float32
SIDE = 8
ROWS = 128
WIDTH = 1024
LINK = 512
TILE = 256
AXES = ("leaf", "col")
VMEM = pl.BlockSpec(memory_space=pltpu.VMEM)
SMEM = pl.BlockSpec(memory_space=pltpu.SMEM)
ANY = pl.BlockSpec(memory_space=pl.ANY)


def lines():
    even = [[(leaf * SIDE + z) * SIDE + y for y in range(SIDE)] for leaf in range(0, 8, 2) for z in range(SIDE)]
    odd = [[(leaf * SIDE + z) * SIDE + y for z in range(SIDE)] for leaf in range(1, 8, 2) for y in range(SIDE)]
    return even + odd


def ring(step):
    pairs = []
    for leaf in range(8):
        for z in range(SIDE):
            for y in range(SIDE):
                dz, dy = (step, 0) if leaf % 2 == 0 else (0, step)
                target = (leaf * SIDE + (z + dz) % SIDE) * SIDE + (y + dy) % SIDE
                pairs.append(((leaf * SIDE + z) * SIDE + y, target))
    return pairs


def swap_cores(value):
    return lax.ppermute(value, "leaf", [(i, i ^ 1) for i in range(8)])


def times_rows(left, right):
    return lax.dot_general(left, right, (((1,), (1,)), ((), ())), preferred_element_type=F32)


def times_lower(left, inverse, out):
    for j in range(WIDTH // TILE):
        depth = TILE * (j + 1)
        rows = inverse[2 * j : 2 * j + 2, :, :, :depth].reshape(TILE, depth)
        out[:, TILE * j : depth] = times_rows(left(depth), rows).astype(BF16)


def child_kernel(row_map, mask, panels, *refs):
    blocks, refs = refs[:9], refs[9:]
    factor, own, sent, inv0, piv, lnk, inv1, p1, x1, x2, f1, r2, f2, placed, contrib, sems = refs
    leaf, col = lax.axis_index("leaf"), lax.axis_index("col")
    core = lax.rem(leaf, 2)
    place = jnp.where(core == 0, col // SIDE, lax.rem(col, SIDE))
    half = SIDE // 2
    sources = [(0, 0, SIDE)] + [(-k, 0, SIDE) for k in (1, 2, 3)] + [(k, 0, SIDE) for k in (1, 2, 3)]
    sources += [(half, 0, half), (half, half, half)]
    copies = [[], [], [], []]
    for i, (block, (offset, first, count)) in enumerate(zip(blocks, sources, strict=True)):
        at = lax.rem(place + offset + SIDE, SIDE)
        for m, target in enumerate((inv0, piv, lnk, inv1)):
            sem = sems.at[i, m]
            by_z = pltpu.make_async_copy(block.at[:, m], target.at[at, pl.ds(first, count)], sem)
            by_y = pltpu.make_async_copy(block.at[:, m], target.at[pl.ds(first, count), at], sem)

            @pl.when(core == 0)
            def _():
                by_z.start()

            @pl.when(core != 0)
            def _():
                by_y.start()

            copies[m].append(by_z)

    zero = jnp.zeros((), BF16)
    x1[:ROWS] = jnp.where(mask[0, 0, 0] != 0, panels[:, :WIDTH], zero)
    x2[:ROWS] = jnp.where(mask[0, 0, 1] != 0, panels[:, WIDTH:], zero)
    placed[...] = jnp.zeros_like(placed)
    for m in (2, 0, 1):
        for copy in copies[m]:
            copy.wait()
    for j in range(LINK // 16):
        one = lnk[j // 4, 2 * j % 8].astype(F32)
        two = lnk[j // 4, 2 * j % 8 + 1].astype(F32)
        x1[ROWS + 16 * j : ROWS + 16 * j + 16] = jnp.concatenate([one[:8], two[:8]], 0).astype(BF16)
        x2[ROWS + 16 * j : ROWS + 16 * j + 16] = jnp.concatenate([one[8:], two[8:]], 0).astype(BF16)
    times_lower(lambda depth: piv[:, :, :, :depth].reshape(WIDTH, depth), inv0, p1)
    times_lower(lambda depth: x1[:, :depth], inv0, f1)
    for j in range(WIDTH // TILE):
        at = slice(TILE * j, TILE * j + TILE)
        r2[:, at] = (x2[:, at].astype(F32) - times_rows(f1[...], p1[at, :])).astype(BF16)
    for copy in copies[3]:
        copy.wait()
    times_lower(lambda depth: r2[:, :depth], inv1, f2)
    contrib[...] = -(times_rows(f1[:ROWS], f1[ROWS:]) + times_rows(f2[:ROWS], f2[ROWS:]))
    factor[:, :WIDTH] = f1[:ROWS]
    factor[:, WIDTH:] = f2[:ROWS]
    flip = core * ROWS

    def put(r, carry):
        t = row_map[0, r]
        t = jnp.where(t >= ROWS, t - ROWS + (ROWS - flip), t + flip)
        placed[pl.ds(t, 1), :] = contrib[pl.ds(r, 1), :]
        return carry

    lax.fori_loop(0, ROWS, put, 0)
    own[...] = placed[:ROWS]
    sent[...] = placed[ROWS:]


def start_from(core, low, high, pairs):
    copies = []
    for from_low, lanes, target, sem in pairs:
        mine, theirs = (low, high) if from_low else (high, low)
        here = pltpu.make_async_copy(mine.at[:, :, :, lanes], target, sem)
        there = pltpu.make_async_copy(theirs.at[:, :, :, lanes], target, sem)

        @pl.when(core == 0)
        def _():
            here.start()

        @pl.when(core != 0)
        def _():
            there.start()

        copies.append(here)
    return copies


def pivot_kernel(mine, theirs, p1, inv0, piv, sems):
    core = lax.rem(lax.axis_index("leaf"), 2)
    half = WIDTH // 2
    tail = pl.ds(WIDTH, half)
    copies = start_from(
        core,
        mine,
        theirs,
        [
            (True, pl.ds(0, WIDTH), inv0, sems.at[0]),
            (True, tail, piv.at[:, :, :, pl.ds(0, half)], sems.at[1]),
            (False, tail, piv.at[:, :, :, pl.ds(half, half)], sems.at[2]),
        ],
    )
    for copy in copies:
        copy.wait()
    times_lower(lambda depth: piv[:, :, :, :depth].reshape(WIDTH, depth), inv0, p1)


def parent_kernel(panels, own, received, p1, mine, theirs, factor, inv0, inv1, x1, f1, r2, f2, sems):
    core = lax.rem(lax.axis_index("leaf"), 2)
    whole = pl.ds(0, WIDTH)
    copies = start_from(
        core, mine, theirs, [(True, whole, inv0, sems.at[0]), (False, whole, inv1, sems.at[1])]
    )
    even = core == 0
    left = jnp.where(even, own[...], received[...])
    right = jnp.where(even, received[...], own[...])
    x1[:, :LINK] = (panels[:, :LINK].astype(F32) + left).astype(BF16)
    x1[:, LINK:] = (panels[:, LINK:WIDTH].astype(F32) + right).astype(BF16)
    copies[0].wait()
    times_lower(lambda depth: x1[:, :depth], inv0, f1)
    for j in range(WIDTH // TILE):
        at = slice(TILE * j, TILE * j + TILE)
        source = panels[:, WIDTH + TILE * j : WIDTH + TILE * j + TILE].astype(F32)
        r2[:, at] = (source - times_rows(f1[...], p1[at, :])).astype(BF16)
    copies[1].wait()
    times_lower(lambda depth: r2[:, :depth], inv1, f2)
    factor[:, :WIDTH] = f1[...]
    factor[:, WIDTH:] = f2[...]


def matrix(*shape, dtype=BF16):
    return pltpu.VMEM(shape, dtype)


def call(kernel, in_specs, outs, scratch, flops):
    return pl.pallas_call(
        kernel,
        in_specs=in_specs,
        out_specs=tuple(VMEM for _ in outs),
        out_shape=tuple(jax.ShapeDtypeStruct(shape, dtype) for shape, dtype in outs),
        scratch_shapes=scratch,
        compiler_params=pltpu.CompilerParams(vmem_limit_bytes=24 << 20),
        cost_estimate=pl.CostEstimate(flops=flops, bytes_accessed=8 << 20, transcendentals=0),
    )


def local(
    child_panels,
    child_links,
    child_pivots,
    child_inverse,
    block_mask,
    row_map,
    parent_panels,
    parent_pivots,
    parent_inverse,
):
    leaf = lax.axis_index("leaf")
    core, parent = leaf % 2, leaf // 2
    half = WIDTH // 2
    my_inverse = lax.dynamic_slice(parent_inverse, (parent, core, 0, 0), (1, 1, 16, WIDTH))[0, 0]
    my_pivots = lax.dynamic_slice(parent_pivots, (parent, 0, core * half), (1, 16, half))[0]
    packed = jnp.concatenate([my_inverse, my_pivots], 1)
    links = jnp.concatenate([child_links[0, :, :WIDTH], child_links[0, :, WIDTH:]], 0)
    message = jnp.stack([child_inverse[0, 0], child_pivots[0], links, child_inverse[0, 1]], 0)
    packed, message = lax.optimization_barrier((packed, message))

    gathered = lax.all_gather(packed, "col", axis=0, tiled=False)
    block = lax.all_to_all(
        jnp.broadcast_to(message[None], (SIDE, *message.shape)), AXES, 0, 0, axis_index_groups=lines()
    )
    up = functools.partial(lax.ppermute, axis_name=AXES, perm=ring(1))
    down = functools.partial(lax.ppermute, axis_name=AXES, perm=ring(-1))
    ups, downs = [block], [block]
    for _ in range(3):
        ups.append(up(ups[-1]))
        downs.append(down(downs[-1]))
    last_up, last_down = up(ups[-1][: SIDE // 2]), down(downs[-1][SIDE // 2 :])

    weight = (SIDE, SIDE, 16, WIDTH)
    stack = ROWS + LINK
    child_factor, own, sent = call(
        child_kernel,
        [SMEM, SMEM, VMEM] + [ANY] * 9,
        [((ROWS, 2 * WIDTH), BF16), ((ROWS, LINK), F32), ((ROWS, LINK), F32)],
        [matrix(*weight)] * 4
        + [matrix(WIDTH, WIDTH)]
        + [matrix(stack, WIDTH)] * 5
        + [matrix(2 * ROWS, LINK, dtype=F32), matrix(ROWS, LINK, dtype=F32), pltpu.SemaphoreType.DMA((9, 4))],
        7_000_000_000,
    )(row_map, block_mask, child_panels[0], *ups, *downs[1:], last_up, last_down)
    gathered, sent = lax.optimization_barrier((gathered, sent))
    received = swap_cores(sent)

    mine = gathered.reshape(SIDE, SIDE, 16, WIDTH + half)
    theirs = swap_cores(mine)
    (parent_p1,) = call(
        pivot_kernel,
        [ANY, ANY],
        [((WIDTH, WIDTH), BF16)],
        [matrix(*weight)] * 2 + [pltpu.SemaphoreType.DMA((3,))],
        1_400_000_000,
    )(mine, theirs)
    (parent_factor,) = call(
        parent_kernel,
        [VMEM] * 4 + [ANY, ANY],
        [((ROWS, 2 * WIDTH), BF16)],
        [matrix(*weight)] * 2 + [matrix(ROWS, WIDTH)] * 4 + [pltpu.SemaphoreType.DMA((2,))],
        800_000_000,
    )(parent_panels[0], own, received, parent_p1, mine, theirs)
    return (child_factor[None], parent_factor[None])


def solution(mesh):
    return jax.shard_map(
        local,
        mesh=mesh,
        in_specs=(
            P("leaf", "col", None),
            P("leaf", "col", None),
            P("leaf", "col", None),
            P("leaf", None, "col", None),
            P("leaf", "col", None),
            P("leaf", "col"),
            P("leaf", "col", None),
            P(None, "col", None),
            P(None, None, "col", None),
        ),
        out_specs=(P("leaf", "col", None), P("leaf", "col", None)),
        check_vma=False,
    )
```

```python
import functools

import jax
import jax.numpy as jnp
from jax import lax
from jax.experimental import pallas as pl
from jax.experimental.pallas import tpu as pltpu
from jax.sharding import PartitionSpec as P

BF16, F32 = jnp.bfloat16, jnp.float32
SIDE = 8
ROWS = 128
WIDTH = 1024
LINK = 512
TILE = 256
AXES = ("leaf", "col")
VMEM = pl.BlockSpec(memory_space=pltpu.VMEM)
SMEM = pl.BlockSpec(memory_space=pltpu.SMEM)
ANY = pl.BlockSpec(memory_space=pl.ANY)
HBM = pl.BlockSpec(memory_space=pltpu.HBM)


def lines():
    even = [[(leaf * SIDE + z) * SIDE + y for y in range(SIDE)] for leaf in range(0, 8, 2) for z in range(SIDE)]
    odd = [[(leaf * SIDE + z) * SIDE + y for z in range(SIDE)] for leaf in range(1, 8, 2) for y in range(SIDE)]
    return even + odd


def ring(step):
    pairs = []
    for leaf in range(8):
        for z in range(SIDE):
            for y in range(SIDE):
                dz, dy = (step, 0) if leaf % 2 == 0 else (0, step)
                target = (leaf * SIDE + (z + dz) % SIDE) * SIDE + (y + dy) % SIDE
                pairs.append(((leaf * SIDE + z) * SIDE + y, target))
    return pairs


def swap_cores(value):
    return lax.ppermute(value, "leaf", [(i, i ^ 1) for i in range(8)])


def times_rows(left, right):
    return lax.dot_general(left, right, (((1,), (1,)), ((), ())), preferred_element_type=F32)


def times_lower(left, inverse, out):
    for j in range(WIDTH // TILE):
        depth = TILE * (j + 1)
        rows = inverse[2 * j : 2 * j + 2, :, :, :depth].reshape(TILE, depth)
        out[:, TILE * j : depth] = times_rows(left(depth), rows).astype(BF16)


def first_kernel(mask, panels, *refs):
    blocks, refs = refs[:9], refs[9:]
    f1, r2, inv0, piv, lnk, p1, x1, x2, sems = refs
    leaf, col = lax.axis_index("leaf"), lax.axis_index("col")
    core = lax.rem(leaf, 2)
    place = jnp.where(core == 0, col // SIDE, lax.rem(col, SIDE))
    half = SIDE // 2
    sources = [(0, 0, SIDE)] + [(-k, 0, SIDE) for k in (1, 2, 3)] + [(k, 0, SIDE) for k in (1, 2, 3)]
    sources += [(half, 0, half), (half, half, half)]
    copies = [[], [], []]
    for i, (block, (offset, first, count)) in enumerate(zip(blocks, sources, strict=True)):
        at = lax.rem(place + offset + SIDE, SIDE)
        for m, target in enumerate((inv0, piv, lnk)):
            sem = sems.at[i, m]
            by_z = pltpu.make_async_copy(block.at[:, m], target.at[at, pl.ds(first, count)], sem)
            by_y = pltpu.make_async_copy(block.at[:, m], target.at[pl.ds(first, count), at], sem)

            @pl.when(core == 0)
            def _():
                by_z.start()

            @pl.when(core != 0)
            def _():
                by_y.start()

            copies[m].append(by_z)

    zero = jnp.zeros((), BF16)
    x1[:ROWS] = jnp.where(mask[0, 0, 0] != 0, panels[:, :WIDTH], zero)
    x2[:ROWS] = jnp.where(mask[0, 0, 1] != 0, panels[:, WIDTH:], zero)
    for m in (2, 0, 1):
        for copy in copies[m]:
            copy.wait()
    for j in range(LINK // 16):
        one = lnk[j // 4, 2 * j % 8].astype(F32)
        two = lnk[j // 4, 2 * j % 8 + 1].astype(F32)
        x1[ROWS + 16 * j : ROWS + 16 * j + 16] = jnp.concatenate([one[:8], two[:8]], 0).astype(BF16)
        x2[ROWS + 16 * j : ROWS + 16 * j + 16] = jnp.concatenate([one[8:], two[8:]], 0).astype(BF16)
    times_lower(lambda depth: piv[:, :, :, :depth].reshape(WIDTH, depth), inv0, p1)
    times_lower(lambda depth: x1[:, :depth], inv0, f1)
    for j in range(WIDTH // TILE):
        at = slice(TILE * j, TILE * j + TILE)
        r2[:, at] = (x2[:, at].astype(F32) - times_rows(f1[...], p1[at, :])).astype(BF16)


def second_kernel(row_map, f1, r2, gathered, factor, own, sent, inv1, f2, placed, contrib, sem):
    copy = pltpu.make_async_copy(gathered.at[:, :, :, pl.ds(0, WIDTH)], inv1, sem)
    copy.start()
    core = lax.rem(lax.axis_index("leaf"), 2)
    placed[...] = jnp.zeros_like(placed)
    factor[:, :WIDTH] = f1[:ROWS]
    contrib[...] = times_rows(f1[:ROWS], f1[ROWS:])
    copy.wait()
    times_lower(lambda depth: r2[:, :depth], inv1, f2)
    contrib[...] = -(contrib[...] + times_rows(f2[:ROWS], f2[ROWS:]))
    factor[:, WIDTH:] = f2[:ROWS]
    flip = core * ROWS

    def put(r, carry):
        t = row_map[0, r]
        t = jnp.where(t >= ROWS, t - flip, t + flip)
        placed[pl.ds(t, 1), :] = contrib[pl.ds(r, 1), :]
        return carry

    lax.fori_loop(0, ROWS, put, 0, unroll=8)
    own[...] = placed[:ROWS]
    sent[...] = placed[ROWS:]


def start_from(core, low, high, pairs):
    copies = []
    for from_low, lanes, target, sem in pairs:
        mine, theirs = (low, high) if from_low else (high, low)
        here = pltpu.make_async_copy(mine.at[:, :, :, lanes], target, sem)
        there = pltpu.make_async_copy(theirs.at[:, :, :, lanes], target, sem)

        @pl.when(core == 0)
        def _():
            here.start()

        @pl.when(core != 0)
        def _():
            there.start()

        copies.append(here)
    return copies


def pivot_kernel(mine, theirs, p1, inv0, piv, sems):
    core = lax.rem(lax.axis_index("leaf"), 2)
    half = WIDTH // 2
    tail = pl.ds(2 * WIDTH, half)
    copies = start_from(
        core,
        mine,
        theirs,
        [
            (True, pl.ds(WIDTH, WIDTH), inv0, sems.at[0]),
            (True, tail, piv.at[:, :, :, pl.ds(0, half)], sems.at[1]),
            (False, tail, piv.at[:, :, :, pl.ds(half, half)], sems.at[2]),
        ],
    )
    for copy in copies:
        copy.wait()
    times_lower(lambda depth: piv[:, :, :, :depth].reshape(WIDTH, depth), inv0, p1)


def parent_kernel(panels, own, received, p1, mine, theirs, factor, inv0, inv1, x1, f1, r2, f2, sems):
    core = lax.rem(lax.axis_index("leaf"), 2)
    whole = pl.ds(WIDTH, WIDTH)
    copies = start_from(
        core, mine, theirs, [(True, whole, inv0, sems.at[0]), (False, whole, inv1, sems.at[1])]
    )
    even = core == 0
    left = jnp.where(even, own[...], received[...])
    right = jnp.where(even, received[...], own[...])
    x1[:, :LINK] = (panels[:, :LINK].astype(F32) + left).astype(BF16)
    x1[:, LINK:] = (panels[:, LINK:WIDTH].astype(F32) + right).astype(BF16)
    copies[0].wait()
    times_lower(lambda depth: x1[:, :depth], inv0, f1)
    for j in range(WIDTH // TILE):
        at = slice(TILE * j, TILE * j + TILE)
        source = panels[:, WIDTH + TILE * j : WIDTH + TILE * j + TILE].astype(F32)
        r2[:, at] = (source - times_rows(f1[...], p1[at, :])).astype(BF16)
    copies[1].wait()
    times_lower(lambda depth: r2[:, :depth], inv1, f2)
    factor[:, :WIDTH] = f1[...]
    factor[:, WIDTH:] = f2[...]


def matrix(*shape, dtype=BF16):
    return pltpu.VMEM(shape, dtype)


def call(kernel, in_specs, outs, scratch, flops, vmem=24):
    return pl.pallas_call(
        kernel,
        in_specs=in_specs,
        out_specs=tuple(VMEM for _ in outs),
        out_shape=tuple(jax.ShapeDtypeStruct(shape, dtype) for shape, dtype in outs),
        scratch_shapes=scratch,
        compiler_params=pltpu.CompilerParams(vmem_limit_bytes=vmem << 20),
        cost_estimate=pl.CostEstimate(flops=flops, bytes_accessed=8 << 20, transcendentals=0),
    )


def local(
    child_panels,
    child_links,
    child_pivots,
    child_inverse,
    block_mask,
    row_map,
    parent_panels,
    parent_pivots,
    parent_inverse,
):
    leaf = lax.axis_index("leaf")
    core, parent = leaf % 2, leaf // 2
    half = WIDTH // 2
    my_inverse = lax.dynamic_slice(parent_inverse, (parent, core, 0, 0), (1, 1, 16, WIDTH))[0, 0]
    my_pivots = lax.dynamic_slice(parent_pivots, (parent, 0, core * half), (1, 16, half))[0]
    packed = jnp.concatenate([child_inverse[0, 1], my_inverse, my_pivots], 1)
    links = jnp.concatenate([child_links[0, :, :WIDTH], child_links[0, :, WIDTH:]], 0)
    message = jnp.stack([child_inverse[0, 0], child_pivots[0], links], 0)
    packed, message = lax.optimization_barrier((packed, message))

    gathered = lax.all_gather(packed, "col", axis=0, tiled=False)
    block = lax.all_to_all(
        jnp.broadcast_to(message[None], (SIDE, *message.shape)), AXES, 0, 0, axis_index_groups=lines()
    )
    up = functools.partial(lax.ppermute, axis_name=AXES, perm=ring(1))
    down = functools.partial(lax.ppermute, axis_name=AXES, perm=ring(-1))
    ups, downs = [block], [block]
    for _ in range(3):
        ups.append(up(ups[-1]))
        downs.append(down(downs[-1]))
    last_up, last_down = up(ups[-1][: SIDE // 2]), down(downs[-1][SIDE // 2 :])

    weight = (SIDE, SIDE, 16, WIDTH)
    stack = ROWS + LINK
    f1, r2 = call(
        first_kernel,
        [SMEM, VMEM] + [ANY] * 9,
        [((stack, WIDTH), BF16)] * 2,
        [matrix(*weight)] * 3 + [matrix(WIDTH, WIDTH)] + [matrix(stack, WIDTH)] * 2 + [pltpu.SemaphoreType.DMA((9, 3))],
        5_000_000_000,
    )(block_mask, child_panels[0], *ups, *downs[1:], last_up, last_down)
    gathered, f1, r2 = lax.optimization_barrier((gathered, f1, r2))
    mine = gathered.reshape(SIDE, SIDE, 16, 2 * WIDTH + half)
    theirs = swap_cores(mine)
    child_factor, own, sent = call(
        second_kernel,
        [SMEM, VMEM, VMEM, HBM],
        [((ROWS, 2 * WIDTH), BF16), ((ROWS, LINK), F32), ((ROWS, LINK), F32)],
        [matrix(*weight), matrix(stack, WIDTH), matrix(2 * ROWS, LINK, dtype=F32), matrix(ROWS, LINK, dtype=F32)]
        + [pltpu.SemaphoreType.DMA(())],
        1_500_000_000,
        52,
    )(row_map, f1, r2, mine)
    received = swap_cores(sent)
    (parent_p1,) = call(
        pivot_kernel,
        [HBM, ANY],
        [((WIDTH, WIDTH), BF16)],
        [matrix(*weight)] * 2 + [pltpu.SemaphoreType.DMA((3,))],
        1_400_000_000,
        36,
    )(mine, theirs)
    (parent_factor,) = call(
        parent_kernel,
        [VMEM] * 4 + [HBM, ANY],
        [((ROWS, 2 * WIDTH), BF16)],
        [matrix(*weight)] * 2 + [matrix(ROWS, WIDTH)] * 4 + [pltpu.SemaphoreType.DMA((2,))],
        800_000_000,
        36,
    )(parent_panels[0], own, received, parent_p1, mine, theirs)
    return (child_factor[None], parent_factor[None])


def solution(mesh):
    return jax.shard_map(
        local,
        mesh=mesh,
        in_specs=(
            P("leaf", "col", None),
            P("leaf", "col", None),
            P("leaf", "col", None),
            P("leaf", None, "col", None),
            P("leaf", "col", None),
            P("leaf", "col"),
            P("leaf", "col", None),
            P(None, "col", None),
            P(None, None, "col", None),
        ),
        out_specs=(P("leaf", "col", None), P("leaf", "col", None)),
        check_vma=False,
    )
```

```python
import functools

import jax
import jax.numpy as jnp
from jax import lax
from jax.experimental import pallas as pl
from jax.experimental.pallas import tpu as pltpu
from jax.sharding import PartitionSpec as P

BF16, F32 = jnp.bfloat16, jnp.float32
SIDE = 8
ROWS = 128
WIDTH = 1024
LINK = 512
TILE = 256
AXES = ("leaf", "col")
VMEM = pl.BlockSpec(memory_space=pltpu.VMEM)
SMEM = pl.BlockSpec(memory_space=pltpu.SMEM)
ANY = pl.BlockSpec(memory_space=pl.ANY)


def lines():
    even = [[(leaf * SIDE + z) * SIDE + y for y in range(SIDE)] for leaf in range(0, 8, 2) for z in range(SIDE)]
    odd = [[(leaf * SIDE + z) * SIDE + y for z in range(SIDE)] for leaf in range(1, 8, 2) for y in range(SIDE)]
    return even + odd


def ring(step):
    pairs = []
    for leaf in range(8):
        for z in range(SIDE):
            for y in range(SIDE):
                dz, dy = (step, 0) if leaf % 2 == 0 else (0, step)
                target = (leaf * SIDE + (z + dz) % SIDE) * SIDE + (y + dy) % SIDE
                pairs.append(((leaf * SIDE + z) * SIDE + y, target))
    return pairs


def swap_cores(value):
    return lax.ppermute(value, "leaf", [(i, i ^ 1) for i in range(8)])


def times_rows(left, right):
    return lax.dot_general(left, right, (((1,), (1,)), ((), ())), preferred_element_type=F32)


def times_lower(left, inverse, out):
    for j in range(WIDTH // TILE):
        depth = TILE * (j + 1)
        rows = inverse[2 * j : 2 * j + 2, :, :, :depth].reshape(TILE, depth)
        out[:, TILE * j : depth] = times_rows(left(depth), rows).astype(BF16)


def pack_kernel(links, pivots, inverse, upper_pivots, upper_inverse, out, low, sems):
    leaf = lax.axis_index("leaf")
    core, parent = lax.rem(leaf, 2), leaf // 2
    half = WIDTH // 2
    part = upper_pivots.at[parent, :, pl.ds(pl.multiple_of(core * half, half), half)]
    pairs = [
        (links.at[0], low),
        (inverse.at[0, 0], out.at[:, pl.ds(0, WIDTH)]),
        (pivots.at[0], out.at[:, pl.ds(WIDTH, WIDTH)]),
        (inverse.at[0, 1], out.at[:, pl.ds(3 * WIDTH, WIDTH)]),
        (upper_inverse.at[parent, core], out.at[:, pl.ds(4 * WIDTH, WIDTH)]),
        (part, out.at[:, pl.ds(5 * WIDTH, half)]),
    ]
    copies = [pltpu.make_async_copy(source, target, sems.at[i]) for i, (source, target) in enumerate(pairs)]
    for copy in copies:
        copy.start()
    copies[0].wait()
    rows = low[...].astype(F32)
    out[:, 2 * WIDTH : 3 * WIDTH] = jnp.concatenate([rows[:, :WIDTH], rows[:, WIDTH:]], 0).astype(BF16)
    for copy in copies[1:]:
        copy.wait()


def arrivals(blocks, targets, sems):
    leaf, col = lax.axis_index("leaf"), lax.axis_index("col")
    core = lax.rem(leaf, 2)
    place = jnp.where(core == 0, col // SIDE, lax.rem(col, SIDE))
    copies = [[] for _ in targets]
    for i, (block, offset) in enumerate(zip(blocks, (0, -1, -2, -3, 1, 2, 3, 4), strict=True)):
        at = lax.rem(place + offset + SIDE, SIDE)
        for m, (target, lane) in enumerate(targets):
            source, sem = block.at[:, :, pl.ds(lane, target.shape[3])], sems.at[i, m]
            by_z = pltpu.make_async_copy(source, target.at[at], sem)
            by_y = pltpu.make_async_copy(source, target.at[:, at], sem)

            @pl.when(core == 0)
            def _():
                by_z.start()

            @pl.when(core != 0)
            def _():
                by_y.start()

            copies[m].append(by_z)
    return copies


def order_kernel(*refs):
    blocks, (inv1, mine, sems) = refs[:8], refs[8:]
    for copies in arrivals(blocks, [(inv1, 0), (mine, WIDTH)], sems):
        for copy in copies:
            copy.wait()


def first_kernel(mask, panels, *refs):
    blocks, refs = refs[:8], refs[8:]
    f1, r2, inv0, piv, lnk, p1, x1, x2, sems = refs
    copies = arrivals(blocks, [(inv0, 0), (piv, WIDTH), (lnk, 2 * WIDTH)], sems)
    zero = jnp.zeros((), BF16)
    x1[:ROWS] = jnp.where(mask[0, 0, 0] != 0, panels[:, :WIDTH], zero)
    x2[:ROWS] = jnp.where(mask[0, 0, 1] != 0, panels[:, WIDTH:], zero)
    for m in (2, 0, 1):
        for copy in copies[m]:
            copy.wait()
    for j in range(LINK // 16):
        one = lnk[j // 4, 2 * j % 8].astype(F32)
        two = lnk[j // 4, 2 * j % 8 + 1].astype(F32)
        x1[ROWS + 16 * j : ROWS + 16 * j + 16] = jnp.concatenate([one[:8], two[:8]], 0).astype(BF16)
        x2[ROWS + 16 * j : ROWS + 16 * j + 16] = jnp.concatenate([one[8:], two[8:]], 0).astype(BF16)
    times_lower(lambda depth: piv[:, :, :, :depth].reshape(WIDTH, depth), inv0, p1)
    times_lower(lambda depth: x1[:, :depth], inv0, f1)
    for j in range(WIDTH // TILE):
        at = slice(TILE * j, TILE * j + TILE)
        r2[:, at] = (x2[:, at].astype(F32) - times_rows(f1[...], p1[at, :])).astype(BF16)


def second_kernel(row_map, f1, r2, inv1, factor, own, sent, f2, placed, contrib):
    core = lax.rem(lax.axis_index("leaf"), 2)
    placed[...] = jnp.zeros_like(placed)
    factor[:, :WIDTH] = f1[:ROWS]
    contrib[...] = times_rows(f1[:ROWS], f1[ROWS:])
    times_lower(lambda depth: r2[:, :depth], inv1, f2)
    contrib[...] = -(contrib[...] + times_rows(f2[:ROWS], f2[ROWS:]))
    factor[:, WIDTH:] = f2[:ROWS]
    flip = core * ROWS

    def put(r, carry):
        t = row_map[0, r]
        t = jnp.where(t >= ROWS, t - flip, t + flip)
        placed[pl.ds(t, 1), :] = contrib[pl.ds(r, 1), :]
        return carry

    lax.fori_loop(0, ROWS, put, 0, unroll=8)
    own[...] = placed[:ROWS]
    sent[...] = placed[ROWS:]


def start_from(core, low, high, pairs):
    copies = []
    for from_low, lanes, target, sem in pairs:
        mine, theirs = (low, high) if from_low else (high, low)
        here = pltpu.make_async_copy(mine.at[:, :, :, lanes], target, sem)
        there = pltpu.make_async_copy(theirs.at[:, :, :, lanes], target, sem)

        @pl.when(core == 0)
        def _():
            here.start()

        @pl.when(core != 0)
        def _():
            there.start()

        copies.append(here)
    return copies


def pivot_kernel(mine, theirs, p1, inv0, piv, sems):
    core = lax.rem(lax.axis_index("leaf"), 2)
    half = WIDTH // 2
    tail = pl.ds(WIDTH, half)
    copies = start_from(
        core,
        mine,
        theirs,
        [
            (True, pl.ds(0, WIDTH), inv0, sems.at[0]),
            (True, tail, piv.at[:, :, :, pl.ds(0, half)], sems.at[1]),
            (False, tail, piv.at[:, :, :, pl.ds(half, half)], sems.at[2]),
        ],
    )
    for copy in copies:
        copy.wait()
    times_lower(lambda depth: piv[:, :, :, :depth].reshape(WIDTH, depth), inv0, p1)


def parent_kernel(panels, own, received, p1, mine, theirs, factor, inv0, inv1, x1, f1, r2, f2, sems):
    core = lax.rem(lax.axis_index("leaf"), 2)
    whole = pl.ds(0, WIDTH)
    copies = start_from(
        core, mine, theirs, [(True, whole, inv0, sems.at[0]), (False, whole, inv1, sems.at[1])]
    )
    even = core == 0
    left = jnp.where(even, own[...], received[...])
    right = jnp.where(even, received[...], own[...])
    x1[:, :LINK] = (panels[:, :LINK].astype(F32) + left).astype(BF16)
    x1[:, LINK:] = (panels[:, LINK:WIDTH].astype(F32) + right).astype(BF16)
    copies[0].wait()
    times_lower(lambda depth: x1[:, :depth], inv0, f1)
    for j in range(WIDTH // TILE):
        at = slice(TILE * j, TILE * j + TILE)
        source = panels[:, WIDTH + TILE * j : WIDTH + TILE * j + TILE].astype(F32)
        r2[:, at] = (source - times_rows(f1[...], p1[at, :])).astype(BF16)
    copies[1].wait()
    times_lower(lambda depth: r2[:, :depth], inv1, f2)
    factor[:, :WIDTH] = f1[...]
    factor[:, WIDTH:] = f2[...]


def matrix(*shape, dtype=BF16):
    return pltpu.VMEM(shape, dtype)


def call(kernel, in_specs, outs, scratch, flops, vmem=24, out_spec=VMEM):
    return pl.pallas_call(
        kernel,
        in_specs=in_specs,
        out_specs=tuple(out_spec for _ in outs),
        out_shape=tuple(jax.ShapeDtypeStruct(shape, dtype) for shape, dtype in outs),
        scratch_shapes=scratch,
        compiler_params=pltpu.CompilerParams(vmem_limit_bytes=vmem << 20),
        cost_estimate=pl.CostEstimate(flops=flops, bytes_accessed=8 << 20, transcendentals=0),
    )


def local(
    child_panels,
    child_links,
    child_pivots,
    child_inverse,
    block_mask,
    row_map,
    parent_panels,
    parent_pivots,
    parent_inverse,
):
    half = WIDTH // 2
    (message,) = call(
        pack_kernel,
        [ANY] * 5,
        [((16, 5 * WIDTH + half), BF16)],
        [matrix(8, 2 * WIDTH), pltpu.SemaphoreType.DMA((6,))],
        1_000_000,
        60,
    )(child_links, child_pivots, child_inverse, parent_pivots, parent_inverse)
    block = lax.all_to_all(
        jnp.broadcast_to(message[None], (SIDE, *message.shape)), AXES, 0, 0, axis_index_groups=lines()
    )
    up = functools.partial(lax.ppermute, axis_name=AXES, perm=ring(1))
    down = functools.partial(lax.ppermute, axis_name=AXES, perm=ring(-1))
    first, second = block[:, :, : 3 * WIDTH], block[:, :, 3 * WIDTH :]
    first_blocks, second_blocks = [first], [second]
    a, b = (first, first), (second, second)
    for step in range(3):
        a, last = (up(a[0]), down(a[1])), b
        b = (up(b[0]), down(b[1]))
        if step:
            *a, _, _ = lax.optimization_barrier((*a, *last))
        *b, a0, a1 = lax.optimization_barrier((*b, *a))
        first_blocks += [a0, a1]
        second_blocks += list(b)
    last, farthest = lax.optimization_barrier((up(a[0]), down(b[1])))
    first_blocks.append(last)
    first_blocks, second_blocks = (
        [blocks[i] for i in (0, 1, 3, 5, 2, 4, 6)] + blocks[7:] for blocks in (first_blocks, second_blocks)
    )

    weight = (SIDE, SIDE, 16, WIDTH)
    stack = ROWS + LINK
    f1, r2 = call(
        first_kernel,
        [SMEM, VMEM] + [ANY] * 8,
        [((stack, WIDTH), BF16)] * 2,
        [matrix(*weight)] * 3 + [matrix(WIDTH, WIDTH)] + [matrix(stack, WIDTH)] * 2 + [pltpu.SemaphoreType.DMA((8, 3))],
        5_000_000_000,
    )(block_mask, child_panels[0], *first_blocks)
    inv1, mine = call(
        order_kernel,
        [ANY] * 8,
        [(weight, BF16), ((SIDE, SIDE, 16, WIDTH + half), BF16)],
        [pltpu.SemaphoreType.DMA((8, 2))],
        1_000_000,
        16,
        ANY,
    )(*second_blocks, farthest)
    theirs = swap_cores(mine)
    child_factor, own, sent = call(
        second_kernel,
        [SMEM, VMEM, VMEM, VMEM],
        [((ROWS, 2 * WIDTH), BF16), ((ROWS, LINK), F32), ((ROWS, LINK), F32)],
        [matrix(stack, WIDTH), matrix(2 * ROWS, LINK, dtype=F32), matrix(ROWS, LINK, dtype=F32)],
        1_500_000_000,
        24,
    )(row_map, f1, r2, inv1)
    received = swap_cores(sent)
    (parent_p1,) = call(
        pivot_kernel,
        [ANY, ANY],
        [((WIDTH, WIDTH), BF16)],
        [matrix(*weight)] * 2 + [pltpu.SemaphoreType.DMA((3,))],
        1_400_000_000,
        24,
    )(mine, theirs)
    (parent_factor,) = call(
        parent_kernel,
        [VMEM] * 4 + [ANY, ANY],
        [((ROWS, 2 * WIDTH), BF16)],
        [matrix(*weight)] * 2 + [matrix(ROWS, WIDTH)] * 4 + [pltpu.SemaphoreType.DMA((2,))],
        800_000_000,
        24,
    )(parent_panels[0], own, received, parent_p1, mine, theirs)
    return (child_factor[None], parent_factor[None])


def solution(mesh):
    return jax.shard_map(
        local,
        mesh=mesh,
        in_specs=(
            P("leaf", "col", None),
            P("leaf", "col", None),
            P("leaf", "col", None),
            P("leaf", None, "col", None),
            P("leaf", "col", None),
            P("leaf", "col"),
            P("leaf", "col", None),
            P(None, "col", None),
            P(None, None, "col", None),
        ),
        out_specs=(P("leaf", "col", None), P("leaf", "col", None)),
        check_vma=False,
    )
```

```python
import functools

import jax
import jax.numpy as jnp
from jax import lax
from jax.experimental import pallas as pl
from jax.experimental.pallas import tpu as pltpu
from jax.sharding import PartitionSpec as P

BF16, F32 = jnp.bfloat16, jnp.float32
SIDE = 8
ROWS = 128
WIDTH = 1024
LINK = 512
TILE = 256
AXES = ("leaf", "col")
VMEM = pl.BlockSpec(memory_space=pltpu.VMEM)
SMEM = pl.BlockSpec(memory_space=pltpu.SMEM)
ANY = pl.BlockSpec(memory_space=pl.ANY)


def lines():
    even = [[(leaf * SIDE + z) * SIDE + y for y in range(SIDE)] for leaf in range(0, 8, 2) for z in range(SIDE)]
    odd = [[(leaf * SIDE + z) * SIDE + y for z in range(SIDE)] for leaf in range(1, 8, 2) for y in range(SIDE)]
    return even + odd


def ring(step):
    pairs = []
    for leaf in range(8):
        for z in range(SIDE):
            for y in range(SIDE):
                dz, dy = (step, 0) if leaf % 2 == 0 else (0, step)
                target = (leaf * SIDE + (z + dz) % SIDE) * SIDE + (y + dy) % SIDE
                pairs.append(((leaf * SIDE + z) * SIDE + y, target))
    return pairs


def swap_cores(value):
    return lax.ppermute(value, "leaf", [(i, i ^ 1) for i in range(8)])


def times_rows(left, right):
    return lax.dot_general(left, right, (((1,), (1,)), ((), ())), preferred_element_type=F32)


def times_lower(left, inverse, out):
    for j in range(WIDTH // TILE):
        depth = TILE * (j + 1)
        rows = inverse[2 * j : 2 * j + 2, :, :, :depth].reshape(TILE, depth)
        out[:, TILE * j : depth] = times_rows(left(depth), rows).astype(BF16)


def pack_kernel(links, pivots, inverse, upper_pivots, upper_inverse, copied, out, low, sems):
    leaf = lax.axis_index("leaf")
    core, parent = lax.rem(leaf, 2), leaf // 2
    half = WIDTH // 2
    part = upper_pivots.at[parent, :, pl.ds(pl.multiple_of(core * half, half), half)]
    pairs = [
        (links.at[0], low),
        (inverse.at[0, 0], out.at[:, pl.ds(0, WIDTH)]),
        (pivots.at[0], out.at[:, pl.ds(WIDTH, WIDTH)]),
        (inverse.at[0, 1], out.at[:, pl.ds(3 * WIDTH, WIDTH)]),
        (upper_inverse.at[parent, core], out.at[:, pl.ds(4 * WIDTH, WIDTH)]),
        (part, out.at[:, pl.ds(5 * WIDTH, half)]),
    ]
    copies = [pltpu.make_async_copy(source, target, sems.at[i]) for i, (source, target) in enumerate(pairs)]
    for copy in copies:
        copy.start()
    copies[0].wait()
    rows = low[...].astype(F32)
    out[:, 2 * WIDTH : 3 * WIDTH] = jnp.concatenate([rows[:, :WIDTH], rows[:, WIDTH:]], 0).astype(BF16)
    for copy in copies[1:]:
        copy.wait()
    for i in range(SIDE):
        copied[i] = out[...]


def arrivals(blocks, targets, sems):
    leaf, col = lax.axis_index("leaf"), lax.axis_index("col")
    core = lax.rem(leaf, 2)
    place = jnp.where(core == 0, col // SIDE, lax.rem(col, SIDE))
    copies = [[] for _ in targets]
    for i, (block, offset) in enumerate(zip(blocks, (0, -1, -2, -3, 1, 2, 3, 4), strict=True)):
        at = lax.rem(place + offset + SIDE, SIDE)
        for m, (target, lane) in enumerate(targets):
            source, sem = block.at[:, :, pl.ds(lane, target.shape[3])], sems.at[i, m]
            by_z = pltpu.make_async_copy(source, target.at[at], sem)
            by_y = pltpu.make_async_copy(source, target.at[:, at], sem)

            @pl.when(core == 0)
            def _():
                by_z.start()

            @pl.when(core != 0)
            def _():
                by_y.start()

            copies[m].append(by_z)
    return copies


def order_kernel(*refs):
    blocks, (inv1, mine, sems) = refs[:8], refs[8:]
    for copies in arrivals(blocks, [(inv1, 0), (mine, WIDTH)], sems):
        for copy in copies:
            copy.wait()


def first_kernel(mask, panels, *refs):
    blocks, refs = refs[:8], refs[8:]
    f1, r2, inv0, piv, lnk, p1, x1, x2, sems = refs
    copies = arrivals(blocks, [(inv0, 0), (piv, WIDTH), (lnk, 2 * WIDTH)], sems)
    zero = jnp.zeros((), BF16)
    x1[:ROWS] = jnp.where(mask[0, 0, 0] != 0, panels[:, :WIDTH], zero)
    x2[:ROWS] = jnp.where(mask[0, 0, 1] != 0, panels[:, WIDTH:], zero)
    for m in (2, 0, 1):
        for copy in copies[m]:
            copy.wait()
    for j in range(LINK // 16):
        one = lnk[j // 4, 2 * j % 8].astype(F32)
        two = lnk[j // 4, 2 * j % 8 + 1].astype(F32)
        x1[ROWS + 16 * j : ROWS + 16 * j + 16] = jnp.concatenate([one[:8], two[:8]], 0).astype(BF16)
        x2[ROWS + 16 * j : ROWS + 16 * j + 16] = jnp.concatenate([one[8:], two[8:]], 0).astype(BF16)
    times_lower(lambda depth: piv[:, :, :, :depth].reshape(WIDTH, depth), inv0, p1)
    times_lower(lambda depth: x1[:, :depth], inv0, f1)
    for j in range(WIDTH // TILE):
        at = slice(TILE * j, TILE * j + TILE)
        r2[:, at] = (x2[:, at].astype(F32) - times_rows(f1[...], p1[at, :])).astype(BF16)


def second_kernel(row_map, f1, r2, inv1, factor, own, sent, f2, placed, contrib):
    core = lax.rem(lax.axis_index("leaf"), 2)
    placed[...] = jnp.zeros_like(placed)
    factor[:, :WIDTH] = f1[:ROWS]
    contrib[...] = times_rows(f1[:ROWS], f1[ROWS:])
    times_lower(lambda depth: r2[:, :depth], inv1, f2)
    contrib[...] = -(contrib[...] + times_rows(f2[:ROWS], f2[ROWS:]))
    factor[:, WIDTH:] = f2[:ROWS]
    flip = core * ROWS

    def put(r, carry):
        t = row_map[0, r]
        t = jnp.where(t >= ROWS, t - flip, t + flip)
        placed[pl.ds(t, 1), :] = contrib[pl.ds(r, 1), :]
        return carry

    lax.fori_loop(0, ROWS, put, 0, unroll=8)
    own[...] = placed[:ROWS]
    sent[...] = placed[ROWS:]


def start_from(core, low, high, pairs):
    copies = []
    for from_low, lanes, target, sem in pairs:
        mine, theirs = (low, high) if from_low else (high, low)
        here = pltpu.make_async_copy(mine.at[:, :, :, lanes], target, sem)
        there = pltpu.make_async_copy(theirs.at[:, :, :, lanes], target, sem)

        @pl.when(core == 0)
        def _():
            here.start()

        @pl.when(core != 0)
        def _():
            there.start()

        copies.append(here)
    return copies


def pivot_kernel(mine, theirs, p1, inv0, inv1, piv, sems):
    core = lax.rem(lax.axis_index("leaf"), 2)
    half = WIDTH // 2
    tail = pl.ds(WIDTH, half)
    copies = start_from(
        core,
        mine,
        theirs,
        [
            (True, pl.ds(0, WIDTH), inv0, sems.at[0]),
            (True, tail, piv.at[:, :, :, pl.ds(0, half)], sems.at[1]),
            (False, tail, piv.at[:, :, :, pl.ds(half, half)], sems.at[2]),
            (False, pl.ds(0, WIDTH), inv1, sems.at[3]),
        ],
    )
    for copy in copies[:3]:
        copy.wait()
    times_lower(lambda depth: piv[:, :, :, :depth].reshape(WIDTH, depth), inv0, p1)
    copies[3].wait()


def parent_kernel(panels, own, received, p1, inv0, inv1, factor, x1, f1, r2, f2):
    core = lax.rem(lax.axis_index("leaf"), 2)
    even = core == 0
    left = jnp.where(even, own[...], received[...])
    right = jnp.where(even, received[...], own[...])
    x1[:, :LINK] = (panels[:, :LINK].astype(F32) + left).astype(BF16)
    x1[:, LINK:] = (panels[:, LINK:WIDTH].astype(F32) + right).astype(BF16)
    times_lower(lambda depth: x1[:, :depth], inv0, f1)
    for j in range(WIDTH // TILE):
        at = slice(TILE * j, TILE * j + TILE)
        source = panels[:, WIDTH + TILE * j : WIDTH + TILE * j + TILE].astype(F32)
        r2[:, at] = (source - times_rows(f1[...], p1[at, :])).astype(BF16)
    times_lower(lambda depth: r2[:, :depth], inv1, f2)
    factor[:, :WIDTH] = f1[...]
    factor[:, WIDTH:] = f2[...]


def matrix(*shape, dtype=BF16):
    return pltpu.VMEM(shape, dtype)


def call(kernel, in_specs, outs, scratch, flops, vmem=24, out_spec=VMEM):
    return pl.pallas_call(
        kernel,
        in_specs=in_specs,
        out_specs=tuple(out_spec for _ in outs),
        out_shape=tuple(jax.ShapeDtypeStruct(shape, dtype) for shape, dtype in outs),
        scratch_shapes=scratch,
        compiler_params=pltpu.CompilerParams(vmem_limit_bytes=vmem << 20),
        cost_estimate=pl.CostEstimate(flops=flops, bytes_accessed=min(flops, 8 << 20), transcendentals=0),
    )


def local(
    child_panels,
    child_links,
    child_pivots,
    child_inverse,
    block_mask,
    row_map,
    parent_panels,
    parent_pivots,
    parent_inverse,
):
    half = WIDTH // 2
    (message,) = call(
        pack_kernel,
        [ANY] * 5,
        [((SIDE, 16, 5 * WIDTH + half), BF16)],
        [matrix(16, 5 * WIDTH + half), matrix(8, 2 * WIDTH), pltpu.SemaphoreType.DMA((6,))],
        1_000_000,
        60,
    )(child_links, child_pivots, child_inverse, parent_pivots, parent_inverse)
    block = lax.all_to_all(message, AXES, 0, 0, axis_index_groups=lines())
    up = functools.partial(lax.ppermute, axis_name=AXES, perm=ring(1))
    down = functools.partial(lax.ppermute, axis_name=AXES, perm=ring(-1))
    first, second = block[:, :, : 3 * WIDTH], block[:, :, 3 * WIDTH :]
    first_blocks, second_blocks = [first], [second]
    a, b = (first, first), (second, second)
    for step in range(3):
        a, last = (up(a[0]), down(a[1])), b
        b = (up(b[0]), down(b[1]))
        if step:
            *a, _, _ = lax.optimization_barrier((*a, *last))
        *b, a0, a1 = lax.optimization_barrier((*b, *a))
        first_blocks += [a0, a1]
        second_blocks += list(b)
    first_blocks.append(up(a[0]))
    farthest = down(b[1])
    first_blocks, second_blocks = (
        [blocks[i] for i in (0, 1, 3, 5, 2, 4, 6)] + blocks[7:] for blocks in (first_blocks, second_blocks)
    )

    weight = (SIDE, SIDE, 16, WIDTH)
    stack = ROWS + LINK
    f1, r2 = call(
        first_kernel,
        [SMEM, VMEM] + [ANY] * 8,
        [((stack, WIDTH), BF16)] * 2,
        [matrix(*weight)] * 3 + [matrix(WIDTH, WIDTH)] + [matrix(stack, WIDTH)] * 2 + [pltpu.SemaphoreType.DMA((8, 3))],
        1_000,
    )(block_mask, child_panels[0], *first_blocks)
    farthest, f1, r2 = lax.optimization_barrier((farthest, f1, r2))
    inv1, mine = call(
        order_kernel,
        [ANY] * 8,
        [(weight, BF16), ((SIDE, SIDE, 16, WIDTH + half), BF16)],
        [pltpu.SemaphoreType.DMA((8, 2))],
        1_000_000,
        16,
        ANY,
    )(*second_blocks, farthest)
    theirs = swap_cores(mine)
    child_factor, own, sent = call(
        second_kernel,
        [SMEM, VMEM, VMEM, VMEM],
        [((ROWS, 2 * WIDTH), BF16), ((ROWS, LINK), F32), ((ROWS, LINK), F32)],
        [matrix(stack, WIDTH), matrix(2 * ROWS, LINK, dtype=F32), matrix(ROWS, LINK, dtype=F32)],
        1_500_000_000,
        24,
    )(row_map, f1, r2, inv1)
    received = swap_cores(sent)
    parent_p1, upper_inv0, upper_inv1 = call(
        pivot_kernel,
        [ANY, ANY],
        [((WIDTH, WIDTH), BF16), (weight, BF16), (weight, BF16)],
        [matrix(*weight), pltpu.SemaphoreType.DMA((4,))],
        1_400_000_000,
    )(mine, theirs)
    (parent_factor,) = call(
        parent_kernel,
        [VMEM] * 6,
        [((ROWS, 2 * WIDTH), BF16)],
        [matrix(ROWS, WIDTH)] * 4,
        800_000_000,
    )(parent_panels[0], own, received, parent_p1, upper_inv0, upper_inv1)
    return (child_factor[None], parent_factor[None])


def solution(mesh):
    return jax.shard_map(
        local,
        mesh=mesh,
        in_specs=(
            P("leaf", "col", None),
            P("leaf", "col", None),
            P("leaf", "col", None),
            P("leaf", None, "col", None),
            P("leaf", "col", None),
            P("leaf", "col"),
            P("leaf", "col", None),
            P(None, "col", None),
            P(None, None, "col", None),
        ),
        out_specs=(P("leaf", "col", None), P("leaf", "col", None)),
        check_vma=False,
    )
```

```python
import functools

import jax
import jax.numpy as jnp
from jax import lax
from jax.experimental import pallas as pl
from jax.experimental.pallas import tpu as pltpu
from jax.sharding import PartitionSpec as P

BF16, F32 = jnp.bfloat16, jnp.float32
SIDE = 8
ROWS = 128
WIDTH = 1024
LINK = 512
TILE = 256
CARRIED = 640
FIRST = CARRIED + 2 * WIDTH
AXES = ("leaf", "col")
VMEM = pl.BlockSpec(memory_space=pltpu.VMEM)
SMEM = pl.BlockSpec(memory_space=pltpu.SMEM)
ANY = pl.BlockSpec(memory_space=pl.ANY)


def lines():
    even = [[(leaf * SIDE + z) * SIDE + y for y in range(SIDE)] for leaf in range(0, 8, 2) for z in range(SIDE)]
    odd = [[(leaf * SIDE + z) * SIDE + y for z in range(SIDE)] for leaf in range(1, 8, 2) for y in range(SIDE)]
    return even + odd


def ring(step):
    pairs = []
    for leaf in range(8):
        for z in range(SIDE):
            for y in range(SIDE):
                dz, dy = (step, 0) if leaf % 2 == 0 else (0, step)
                target = (leaf * SIDE + (z + dz) % SIDE) * SIDE + (y + dy) % SIDE
                pairs.append(((leaf * SIDE + z) * SIDE + y, target))
    return pairs


def swap_cores(value):
    return lax.ppermute(value, "leaf", [(i, i ^ 1) for i in range(8)])


def times_rows(left, right):
    return lax.dot_general(left, right, (((1,), (1,)), ((), ())), preferred_element_type=F32)


def times_lower(left, inverse, out):
    for j in range(WIDTH // TILE):
        depth = TILE * (j + 1)
        rows = inverse[2 * j : 2 * j + 2, :, :, :depth].reshape(TILE, depth)
        out[:, TILE * j : depth] = times_rows(left(depth), rows).astype(BF16)


def lent_kernel(inverse, upper_inverse, out, sems):
    leaf = lax.axis_index("leaf")
    core, parent = lax.rem(leaf, 2), leaf // 2
    units = (inverse.at[0, 0], inverse.at[0, 1], upper_inverse.at[parent, core])
    copies = [
        pltpu.make_async_copy(
            unit.at[:, pl.ds(CARRIED, WIDTH - CARRIED)],
            out.at[:, pl.ds((WIDTH - CARRIED) * i, WIDTH - CARRIED)],
            sems.at[i],
        )
        for i, unit in enumerate(units)
    ]
    for copy in copies:
        copy.start()
    for copy in copies:
        copy.wait()


def pack_kernel(links, pivots, inverse, upper_pivots, upper_inverse, lent, out, low, inv0, inv1, upper, sems):
    leaf, z = lax.axis_index("leaf"), lax.axis_index("col") // SIDE
    core, parent = lax.rem(leaf, 2), leaf // 2
    half = WIDTH // 2
    part = upper_pivots.at[parent, :, pl.ds(pl.multiple_of(core * half, half), half)]
    pairs = [
        (links.at[0], low),
        (inverse.at[0, 0], inv0),
        (inverse.at[0, 1], inv1),
        (upper_inverse.at[parent, core], upper),
        (pivots.at[0], out.at[:, pl.ds(CARRIED, WIDTH)]),
        (part, out.at[:, pl.ds(FIRST + 2 * CARRIED, half)]),
    ]
    copies = [pltpu.make_async_copy(source, target, sems.at[i]) for i, (source, target) in enumerate(pairs)]
    for copy in copies:
        copy.start()
    for copy in copies[:4]:
        copy.wait()
    rows = low[...].astype(F32)
    rows = jnp.concatenate([rows[:, :WIDTH], rows[:, WIDTH:]], 0).astype(BF16)
    out[:, CARRIED + WIDTH : FIRST] = rows
    for i, (unit, at) in enumerate(((inv0, 0), (inv1, FIRST), (upper, FIRST + CARRIED))):
        more = lent[:, (WIDTH - CARRIED) * i : (WIDTH - CARRIED) * (i + 1)]
        out[:, at : at + 256] = unit[:, :256]
        out[:, at + 256 : at + 512] = jnp.where(z < 2, more[:, :256], unit[:, 256:512])
        last = jnp.where(z < 4, more[:, :128], unit[:, 512:CARRIED])
        out[:, at + 512 : at + CARRIED] = jnp.where(z < 2, more[:, 256:], last)
    for copy in copies[4:]:
        copy.wait()


def arrivals(blocks, targets, sems):
    leaf, col = lax.axis_index("leaf"), lax.axis_index("col")
    core = lax.rem(leaf, 2)
    place = jnp.where(core == 0, col // SIDE, lax.rem(col, SIDE))
    by_z, by_y = [[] for _ in targets], [[] for _ in targets]
    for i, (block, offset) in enumerate(zip(blocks, (0, -1, -2, -3, 1, 2, 3, 4), strict=True)):
        at = lax.rem(place + offset + SIDE, SIDE)
        mirror = SIDE - 1 - at
        for m, (target, lane, lanes, triangle) in enumerate(targets):
            if not triangle:
                source = block.at[:, :, pl.ds(lane, lanes)]
                by_z[m].append(pltpu.make_async_copy(source, target.at[at], sems.at[i, m, 0]))
                by_y[m].append(pltpu.make_async_copy(source, target.at[:, at], sems.at[i, m, 0]))
                continue
            second = jnp.where(at < 2, mirror, at), pl.multiple_of(jnp.where(at < 2, 640, 256), 128)
            third = jnp.where(at < 4, mirror, at), pl.multiple_of(jnp.where(at < 2, 896, jnp.where(at < 4, 640, 512)), 128)
            for k, (start, count, (row, to)) in enumerate(
                ((0, 256, (at, 0)), (256, 256, second), (512, 128, third))
            ):
                source = block.at[:, :, pl.ds(lane + start, count)]
                by_z[m].append(
                    pltpu.make_async_copy(source, target.at[row, :, :, pl.ds(to, count)], sems.at[i, m, k])
                )
            pieces = [(0, 8, 0, 0, 256, 0), (2, 6, 2, 256, 256, 256), (4, 4, 4, 512, 128, 512)]
            pieces += [(0, 1, 7, 256, 256, 640), (1, 1, 6, 256, 256, 640), (0, 1, 7, 512, 128, 896)]
            pieces += [(1, 1, 6, 512, 128, 896), (2, 1, 5, 512, 128, 640), (3, 1, 4, 512, 128, 640)]
            for k, (first, rows, row, start, count, to) in enumerate(pieces):
                source = block.at[pl.ds(first, rows), :, pl.ds(lane + start, count)]
                by_y[m].append(
                    pltpu.make_async_copy(
                        source, target.at[pl.ds(row, rows), at, :, pl.ds(to, count)], sems.at[i, m, k]
                    )
                )

    def each(copies, act):
        for copy in copies:
            act(copy)

    def both(lists, act):
        @pl.when(core == 0)
        def _():
            for copies in lists[0]:
                each(copies, act)

        @pl.when(core != 0)
        def _():
            for copies in lists[1]:
                each(copies, act)

    both((by_z, by_y), lambda copy: copy.start())
    return [
        (lambda m=m: both((by_z[m : m + 1], by_y[m : m + 1]), lambda copy: copy.wait())) for m in range(len(targets))
    ]


def order_kernel(*refs):
    blocks, (inv1, mine, sems) = refs[:8], refs[8:]
    tail = mine.at[:, :, :, pl.ds(WIDTH, WIDTH // 2)]
    targets = [(inv1, 0, CARRIED, True), (mine, CARRIED, CARRIED, True), (tail, 2 * CARRIED, WIDTH // 2, False)]
    for wait in arrivals(blocks, targets, sems):
        wait()


def first_kernel(mask, panels, *refs):
    blocks, refs = refs[:8], refs[8:]
    f1, r2, inv0, piv, lnk, p1, x1, x2, sems = refs
    targets = [(inv0, 0, CARRIED, True), (piv, CARRIED, WIDTH, False), (lnk, CARRIED + WIDTH, WIDTH, False)]
    waits = arrivals(blocks, targets, sems)
    zero = jnp.zeros((), BF16)
    x1[:ROWS] = jnp.where(mask[0, 0, 0] != 0, panels[:, :WIDTH], zero)
    x2[:ROWS] = jnp.where(mask[0, 0, 1] != 0, panels[:, WIDTH:], zero)
    for wait in waits:
        wait()
    for j in range(LINK // 16):
        one = lnk[j // 4, 2 * j % 8].astype(F32)
        two = lnk[j // 4, 2 * j % 8 + 1].astype(F32)
        x1[ROWS + 16 * j : ROWS + 16 * j + 16] = jnp.concatenate([one[:8], two[:8]], 0).astype(BF16)
        x2[ROWS + 16 * j : ROWS + 16 * j + 16] = jnp.concatenate([one[8:], two[8:]], 0).astype(BF16)
    times_lower(lambda depth: piv[:, :, :, :depth].reshape(WIDTH, depth), inv0, p1)
    times_lower(lambda depth: x1[:, :depth], inv0, f1)
    for j in range(WIDTH // TILE):
        at = slice(TILE * j, TILE * j + TILE)
        r2[:, at] = (x2[:, at].astype(F32) - times_rows(f1[...], p1[at, :])).astype(BF16)


def second_kernel(row_map, f1, r2, inv1, factor, own, sent, f2, placed, contrib):
    core = lax.rem(lax.axis_index("leaf"), 2)
    placed[...] = jnp.zeros_like(placed)
    factor[:, :WIDTH] = f1[:ROWS]
    contrib[...] = times_rows(f1[:ROWS], f1[ROWS:])
    times_lower(lambda depth: r2[:, :depth], inv1, f2)
    contrib[...] = -(contrib[...] + times_rows(f2[:ROWS], f2[ROWS:]))
    factor[:, WIDTH:] = f2[:ROWS]
    flip = core * ROWS

    def put(r, carry):
        t = row_map[0, r]
        t = jnp.where(t >= ROWS, t - flip, t + flip)
        placed[pl.ds(t, 1), :] = contrib[pl.ds(r, 1), :]
        return carry

    lax.fori_loop(0, ROWS, put, 0, unroll=8)
    own[...] = placed[:ROWS]
    sent[...] = placed[ROWS:]


def start_from(core, low, high, pairs):
    copies = []
    for from_low, lanes, target, sem in pairs:
        mine, theirs = (low, high) if from_low else (high, low)
        here = pltpu.make_async_copy(mine.at[:, :, :, lanes], target, sem)
        there = pltpu.make_async_copy(theirs.at[:, :, :, lanes], target, sem)

        @pl.when(core == 0)
        def _():
            here.start()

        @pl.when(core != 0)
        def _():
            there.start()

        copies.append(here)
    return copies


def pivot_kernel(mine, theirs, p1, inv0, inv1, piv, sems):
    core = lax.rem(lax.axis_index("leaf"), 2)
    half = WIDTH // 2
    tail = pl.ds(WIDTH, half)
    copies = start_from(
        core,
        mine,
        theirs,
        [
            (True, pl.ds(0, WIDTH), inv0, sems.at[0]),
            (True, tail, piv.at[:, :, :, pl.ds(0, half)], sems.at[1]),
            (False, tail, piv.at[:, :, :, pl.ds(half, half)], sems.at[2]),
            (False, pl.ds(0, WIDTH), inv1, sems.at[3]),
        ],
    )
    for copy in copies[:3]:
        copy.wait()
    times_lower(lambda depth: piv[:, :, :, :depth].reshape(WIDTH, depth), inv0, p1)
    copies[3].wait()


def parent_kernel(panels, own, received, p1, inv0, inv1, factor, x1, f1, r2, f2):
    core = lax.rem(lax.axis_index("leaf"), 2)
    even = core == 0
    left = jnp.where(even, own[...], received[...])
    right = jnp.where(even, received[...], own[...])
    x1[:, :LINK] = (panels[:, :LINK].astype(F32) + left).astype(BF16)
    x1[:, LINK:] = (panels[:, LINK:WIDTH].astype(F32) + right).astype(BF16)
    times_lower(lambda depth: x1[:, :depth], inv0, f1)
    for j in range(WIDTH // TILE):
        at = slice(TILE * j, TILE * j + TILE)
        source = panels[:, WIDTH + TILE * j : WIDTH + TILE * j + TILE].astype(F32)
        r2[:, at] = (source - times_rows(f1[...], p1[at, :])).astype(BF16)
    times_lower(lambda depth: r2[:, :depth], inv1, f2)
    factor[:, :WIDTH] = f1[...]
    factor[:, WIDTH:] = f2[...]


def matrix(*shape, dtype=BF16):
    return pltpu.VMEM(shape, dtype)


def call(kernel, in_specs, outs, scratch, flops, vmem=24, out_spec=VMEM):
    return pl.pallas_call(
        kernel,
        in_specs=in_specs,
        out_specs=tuple(out_spec for _ in outs),
        out_shape=tuple(jax.ShapeDtypeStruct(shape, dtype) for shape, dtype in outs),
        scratch_shapes=scratch,
        compiler_params=pltpu.CompilerParams(vmem_limit_bytes=vmem << 20),
        cost_estimate=pl.CostEstimate(flops=flops, bytes_accessed=min(flops, 8 << 20), transcendentals=0),
    )


def local(
    child_panels,
    child_links,
    child_pivots,
    child_inverse,
    block_mask,
    row_map,
    parent_panels,
    parent_pivots,
    parent_inverse,
):
    half = WIDTH // 2
    (lent,) = call(
        lent_kernel,
        [ANY] * 2,
        [((16, 3 * (WIDTH - CARRIED)), BF16)],
        [pltpu.SemaphoreType.DMA((3,))],
        1_000,
        60,
    )(child_inverse, parent_inverse)
    mirrored = [(z * SIDE + y, (SIDE - 1 - z) * SIDE + y) for z in range(SIDE // 2, SIDE) for y in range(SIDE)]
    lent = lax.ppermute(lent, "col", mirrored)
    (message,) = call(
        pack_kernel,
        [ANY] * 5 + [VMEM],
        [((16, FIRST + 2 * CARRIED + half), BF16)],
        [matrix(8, 2 * WIDTH)] + [matrix(16, WIDTH)] * 3 + [pltpu.SemaphoreType.DMA((6,))],
        1_000,
        60,
    )(child_links, child_pivots, child_inverse, parent_pivots, parent_inverse, lent)
    message = jnp.broadcast_to(message[None], (SIDE, *message.shape))
    block = lax.all_to_all(message, AXES, 0, 0, axis_index_groups=lines())
    up = functools.partial(lax.ppermute, axis_name=AXES, perm=ring(1))
    down = functools.partial(lax.ppermute, axis_name=AXES, perm=ring(-1))
    first, second = block[:, :, :FIRST], block[:, :, FIRST:]
    first_blocks, second_blocks = [first], [second]
    a, b = (first, first), (second, second)
    for step in range(3):
        b, last = (up(b[0]), down(b[1])), a
        a = (up(a[0]), down(a[1]))
        if step:
            *b, _, _ = lax.optimization_barrier((*b, *last))
        *a, b0, b1 = lax.optimization_barrier((*a, *b))
        second_blocks += [b0, b1]
        first_blocks += list(a)
    upper_far, lower_far = lax.optimization_barrier((up(b[0]), down(a[1])))
    second_blocks.append(upper_far)
    first_blocks.append(lower_far)
    first_blocks, second_blocks = (
        [blocks[i] for i in (0, 1, 3, 5, 2, 4, 6)] + blocks[7:] for blocks in (first_blocks, second_blocks)
    )

    weight = (SIDE, SIDE, 16, WIDTH)
    stack = ROWS + LINK
    f1, r2 = call(
        first_kernel,
        [SMEM, VMEM] + [ANY] * 8,
        [((stack, WIDTH), BF16)] * 2,
        [matrix(*weight)] * 3 + [matrix(WIDTH, WIDTH)] + [matrix(stack, WIDTH)] * 2 + [pltpu.SemaphoreType.DMA((8, 3, 9))],
        1_000,
    )(block_mask, child_panels[0], *first_blocks)
    inv1, mine = call(
        order_kernel,
        [ANY] * 8,
        [(weight, BF16), ((SIDE, SIDE, 16, WIDTH + half), BF16)],
        [pltpu.SemaphoreType.DMA((8, 3, 9))],
        1_000_000,
        16,
        ANY,
    )(*second_blocks)
    theirs = swap_cores(mine)
    child_factor, own, sent = call(
        second_kernel,
        [SMEM, VMEM, VMEM, VMEM],
        [((ROWS, 2 * WIDTH), BF16), ((ROWS, LINK), F32), ((ROWS, LINK), F32)],
        [matrix(stack, WIDTH), matrix(2 * ROWS, LINK, dtype=F32), matrix(ROWS, LINK, dtype=F32)],
        1_500_000_000,
        24,
    )(row_map, f1, r2, inv1)
    received = swap_cores(sent)
    parent_p1, upper_inv0, upper_inv1 = call(
        pivot_kernel,
        [ANY, ANY],
        [((WIDTH, WIDTH), BF16), (weight, BF16), (weight, BF16)],
        [matrix(*weight), pltpu.SemaphoreType.DMA((4,))],
        1_400_000_000,
    )(mine, theirs)
    (parent_factor,) = call(
        parent_kernel,
        [VMEM] * 6,
        [((ROWS, 2 * WIDTH), BF16)],
        [matrix(ROWS, WIDTH)] * 4,
        800_000_000,
    )(parent_panels[0], own, received, parent_p1, upper_inv0, upper_inv1)
    return (child_factor[None], parent_factor[None])


def solution(mesh):
    return jax.shard_map(
        local,
        mesh=mesh,
        in_specs=(
            P("leaf", "col", None),
            P("leaf", "col", None),
            P("leaf", "col", None),
            P("leaf", None, "col", None),
            P("leaf", "col", None),
            P("leaf", "col"),
            P("leaf", "col", None),
            P(None, "col", None),
            P(None, None, "col", None),
        ),
        out_specs=(P("leaf", "col", None), P("leaf", "col", None)),
        check_vma=False,
    )
```

```python
import functools

import jax
import jax.numpy as jnp
from jax import lax
from jax.experimental import pallas as pl
from jax.experimental.pallas import tpu as pltpu
from jax.sharding import PartitionSpec as P

BF16, F32 = jnp.bfloat16, jnp.float32
SIDE = 8
ROWS = 128
WIDTH = 1024
LINK = 512
TILE = 256
AXES = ("leaf", "col")
VMEM = pl.BlockSpec(memory_space=pltpu.VMEM)
SMEM = pl.BlockSpec(memory_space=pltpu.SMEM)
ANY = pl.BlockSpec(memory_space=pl.ANY)


def lines():
    even = [[(leaf * SIDE + z) * SIDE + y for y in range(SIDE)] for leaf in range(0, 8, 2) for z in range(SIDE)]
    odd = [[(leaf * SIDE + z) * SIDE + y for z in range(SIDE)] for leaf in range(1, 8, 2) for y in range(SIDE)]
    return even + odd


def ring(step):
    pairs = []
    for leaf in range(8):
        for z in range(SIDE):
            for y in range(SIDE):
                dz, dy = (step, 0) if leaf % 2 == 0 else (0, step)
                target = (leaf * SIDE + (z + dz) % SIDE) * SIDE + (y + dy) % SIDE
                pairs.append(((leaf * SIDE + z) * SIDE + y, target))
    return pairs


def swap_cores(value):
    return lax.ppermute(value, "leaf", [(i, i ^ 1) for i in range(8)])


def times_rows(left, right):
    return lax.dot_general(left, right, (((1,), (1,)), ((), ())), preferred_element_type=F32)


def times_lower(left, inverse, out):
    for j in range(WIDTH // TILE):
        depth = TILE * (j + 1)
        rows = inverse[2 * j : 2 * j + 2, :, :, :depth].reshape(TILE, depth)
        out[:, TILE * j : depth] = times_rows(left(depth), rows).astype(BF16)


def pack_kernel(links, pivots, inverse, upper_pivots, upper_inverse, copied, out, low, sems):
    leaf = lax.axis_index("leaf")
    core, parent = lax.rem(leaf, 2), leaf // 2
    half = WIDTH // 2
    part = upper_pivots.at[parent, :, pl.ds(pl.multiple_of(core * half, half), half)]
    pairs = [
        (links.at[0], low),
        (inverse.at[0, 0], out.at[:, pl.ds(0, WIDTH)]),
        (pivots.at[0], out.at[:, pl.ds(WIDTH, WIDTH)]),
        (inverse.at[0, 1], out.at[:, pl.ds(3 * WIDTH, WIDTH)]),
        (upper_inverse.at[parent, core], out.at[:, pl.ds(4 * WIDTH, WIDTH)]),
        (part, out.at[:, pl.ds(5 * WIDTH, half)]),
    ]
    copies = [pltpu.make_async_copy(source, target, sems.at[i]) for i, (source, target) in enumerate(pairs)]
    for copy in copies:
        copy.start()
    copies[0].wait()
    rows = low[...].astype(F32)
    out[:, 2 * WIDTH : 3 * WIDTH] = jnp.concatenate([rows[:, :WIDTH], rows[:, WIDTH:]], 0).astype(BF16)
    for copy in copies[1:]:
        copy.wait()
    for i in range(SIDE):
        copied[i] = out[...]


def arrivals(blocks, targets, sems):
    leaf, col = lax.axis_index("leaf"), lax.axis_index("col")
    core = lax.rem(leaf, 2)
    place = jnp.where(core == 0, col // SIDE, lax.rem(col, SIDE))
    copies = [[] for _ in targets]
    for i, (block, offset) in enumerate(zip(blocks, (0, -1, -2, -3, 1, 2, 3, 4), strict=True)):
        at = lax.rem(place + offset + SIDE, SIDE)
        for m, (target, lane) in enumerate(targets):
            source, sem = block.at[:, :, pl.ds(lane, target.shape[3])], sems.at[i, m]
            by_z = pltpu.make_async_copy(source, target.at[at], sem)
            by_y = pltpu.make_async_copy(source, target.at[:, at], sem)

            @pl.when(core == 0)
            def _():
                by_z.start()

            @pl.when(core != 0)
            def _():
                by_y.start()

            copies[m].append(by_z)
    return copies


def order_kernel(*refs):
    blocks, (inv1, mine, sems) = refs[:8], refs[8:]
    for copies in arrivals(blocks, [(inv1, 0), (mine, WIDTH)], sems):
        for copy in copies:
            copy.wait()


def first_kernel(mask, panels, *refs):
    blocks, refs = refs[:8], refs[8:]
    f1, r2, inv0, piv, lnk, p1, x1, x2, sems = refs
    copies = arrivals(blocks, [(inv0, 0), (piv, WIDTH), (lnk, 2 * WIDTH)], sems)
    zero = jnp.zeros((), BF16)
    x1[:ROWS] = jnp.where(mask[0, 0, 0] != 0, panels[:, :WIDTH], zero)
    x2[:ROWS] = jnp.where(mask[0, 0, 1] != 0, panels[:, WIDTH:], zero)
    for m in (2, 0, 1):
        for copy in copies[m]:
            copy.wait()
    for j in range(LINK // 16):
        one = lnk[j // 4, 2 * j % 8].astype(F32)
        two = lnk[j // 4, 2 * j % 8 + 1].astype(F32)
        x1[ROWS + 16 * j : ROWS + 16 * j + 16] = jnp.concatenate([one[:8], two[:8]], 0).astype(BF16)
        x2[ROWS + 16 * j : ROWS + 16 * j + 16] = jnp.concatenate([one[8:], two[8:]], 0).astype(BF16)
    times_lower(lambda depth: piv[:, :, :, :depth].reshape(WIDTH, depth), inv0, p1)
    times_lower(lambda depth: x1[:, :depth], inv0, f1)
    for j in range(WIDTH // TILE):
        at = slice(TILE * j, TILE * j + TILE)
        r2[:, at] = (x2[:, at].astype(F32) - times_rows(f1[...], p1[at, :])).astype(BF16)


def second_kernel(row_map, f1, r2, inv1, factor, own, sent, f2, placed, contrib):
    core = lax.rem(lax.axis_index("leaf"), 2)
    placed[...] = jnp.zeros_like(placed)
    factor[:, :WIDTH] = f1[:ROWS]
    contrib[...] = times_rows(f1[:ROWS], f1[ROWS:])
    times_lower(lambda depth: r2[:, :depth], inv1, f2)
    contrib[...] = -(contrib[...] + times_rows(f2[:ROWS], f2[ROWS:]))
    factor[:, WIDTH:] = f2[:ROWS]
    flip = core * ROWS

    for r in range(ROWS):
        t = row_map[0, r]
        placed[pl.ds(jnp.where(t >= ROWS, t - flip, t + flip), 1), :] = contrib[r : r + 1, :]
    own[...] = placed[:ROWS]
    sent[...] = placed[ROWS:]


def start_from(core, low, high, pairs):
    copies = []
    for from_low, lanes, target, sem in pairs:
        mine, theirs = (low, high) if from_low else (high, low)
        here = pltpu.make_async_copy(mine.at[:, :, :, lanes], target, sem)
        there = pltpu.make_async_copy(theirs.at[:, :, :, lanes], target, sem)

        @pl.when(core == 0)
        def _():
            here.start()

        @pl.when(core != 0)
        def _():
            there.start()

        copies.append(here)
    return copies


def pivot_kernel(mine, theirs, p1, inv0, inv1, piv, sems):
    core = lax.rem(lax.axis_index("leaf"), 2)
    half = WIDTH // 2
    tail = pl.ds(WIDTH, half)
    copies = start_from(
        core,
        mine,
        theirs,
        [
            (True, pl.ds(0, WIDTH), inv0, sems.at[0]),
            (True, tail, piv.at[:, :, :, pl.ds(0, half)], sems.at[1]),
            (False, tail, piv.at[:, :, :, pl.ds(half, half)], sems.at[2]),
            (False, pl.ds(0, WIDTH), inv1, sems.at[3]),
        ],
    )
    for copy in copies[:3]:
        copy.wait()
    times_lower(lambda depth: piv[:, :, :, :depth].reshape(WIDTH, depth), inv0, p1)
    copies[3].wait()


def parent_kernel(panels, own, received, p1, inv0, inv1, factor, x1, f1, r2, f2):
    core = lax.rem(lax.axis_index("leaf"), 2)
    even = core == 0
    left = jnp.where(even, own[...], received[...])
    right = jnp.where(even, received[...], own[...])
    x1[:, :LINK] = (panels[:, :LINK].astype(F32) + left).astype(BF16)
    x1[:, LINK:] = (panels[:, LINK:WIDTH].astype(F32) + right).astype(BF16)
    times_lower(lambda depth: x1[:, :depth], inv0, f1)
    for j in range(WIDTH // TILE):
        at = slice(TILE * j, TILE * j + TILE)
        source = panels[:, WIDTH + TILE * j : WIDTH + TILE * j + TILE].astype(F32)
        r2[:, at] = (source - times_rows(f1[...], p1[at, :])).astype(BF16)
    times_lower(lambda depth: r2[:, :depth], inv1, f2)
    factor[:, :WIDTH] = f1[...]
    factor[:, WIDTH:] = f2[...]


def matrix(*shape, dtype=BF16):
    return pltpu.VMEM(shape, dtype)


def call(kernel, in_specs, outs, scratch, flops, vmem=24, out_spec=VMEM):
    return pl.pallas_call(
        kernel,
        in_specs=in_specs,
        out_specs=tuple(out_spec for _ in outs),
        out_shape=tuple(jax.ShapeDtypeStruct(shape, dtype) for shape, dtype in outs),
        scratch_shapes=scratch,
        compiler_params=pltpu.CompilerParams(vmem_limit_bytes=vmem << 20),
        cost_estimate=pl.CostEstimate(flops=flops, bytes_accessed=min(flops, 8 << 20), transcendentals=0),
    )


def local(
    child_panels,
    child_links,
    child_pivots,
    child_inverse,
    block_mask,
    row_map,
    parent_panels,
    parent_pivots,
    parent_inverse,
):
    half = WIDTH // 2
    (message,) = call(
        pack_kernel,
        [ANY] * 5,
        [((SIDE, 16, 5 * WIDTH + half), BF16)],
        [matrix(16, 5 * WIDTH + half), matrix(8, 2 * WIDTH), pltpu.SemaphoreType.DMA((6,))],
        1_000_000,
        60,
    )(child_links, child_pivots, child_inverse, parent_pivots, parent_inverse)
    block = lax.all_to_all(message, AXES, 0, 0, axis_index_groups=lines())
    up = functools.partial(lax.ppermute, axis_name=AXES, perm=ring(1))
    down = functools.partial(lax.ppermute, axis_name=AXES, perm=ring(-1))
    first, second = block[:, :, : 3 * WIDTH], block[:, :, 3 * WIDTH :]
    first_blocks, second_blocks = [first], [second]
    a, b = (first, first), (second, second)
    for step in range(3):
        a, last = (up(a[0]), down(a[1])), b
        b = (up(b[0]), down(b[1]))
        if step:
            *a, _, _ = lax.optimization_barrier((*a, *last))
        *b, a0, a1 = lax.optimization_barrier((*b, *a))
        first_blocks += [a0, a1]
        second_blocks += list(b)
    first_blocks.append(up(a[0]))
    farthest = down(b[1])
    first_blocks, second_blocks = (
        [blocks[i] for i in (0, 1, 3, 5, 2, 4, 6)] + blocks[7:] for blocks in (first_blocks, second_blocks)
    )

    weight = (SIDE, SIDE, 16, WIDTH)
    stack = ROWS + LINK
    f1, r2 = call(
        first_kernel,
        [SMEM, VMEM] + [ANY] * 8,
        [((stack, WIDTH), BF16)] * 2,
        [matrix(*weight)] * 3 + [matrix(WIDTH, WIDTH)] + [matrix(stack, WIDTH)] * 2 + [pltpu.SemaphoreType.DMA((8, 3))],
        1_000,
    )(block_mask, child_panels[0], *first_blocks)
    farthest, f1, r2 = lax.optimization_barrier((farthest, f1, r2))
    inv1, mine = call(
        order_kernel,
        [ANY] * 8,
        [(weight, BF16), ((SIDE, SIDE, 16, WIDTH + half), BF16)],
        [pltpu.SemaphoreType.DMA((8, 2))],
        1_000_000,
        16,
        ANY,
    )(*second_blocks, farthest)
    theirs = swap_cores(mine)
    child_factor, own, sent = call(
        second_kernel,
        [SMEM, VMEM, VMEM, VMEM],
        [((ROWS, 2 * WIDTH), BF16), ((ROWS, LINK), F32), ((ROWS, LINK), F32)],
        [matrix(stack, WIDTH), matrix(2 * ROWS, LINK, dtype=F32), matrix(ROWS, LINK, dtype=F32)],
        1_500_000_000,
        24,
    )(row_map, f1, r2, inv1)
    received = swap_cores(sent)
    parent_p1, upper_inv0, upper_inv1 = call(
        pivot_kernel,
        [ANY, ANY],
        [((WIDTH, WIDTH), BF16), (weight, BF16), (weight, BF16)],
        [matrix(*weight), pltpu.SemaphoreType.DMA((4,))],
        1_400_000_000,
    )(mine, theirs)
    (parent_factor,) = call(
        parent_kernel,
        [VMEM] * 6,
        [((ROWS, 2 * WIDTH), BF16)],
        [matrix(ROWS, WIDTH)] * 4,
        800_000_000,
    )(parent_panels[0], own, received, parent_p1, upper_inv0, upper_inv1)
    return (child_factor[None], parent_factor[None])


def solution(mesh):
    return jax.shard_map(
        local,
        mesh=mesh,
        in_specs=(
            P("leaf", "col", None),
            P("leaf", "col", None),
            P("leaf", "col", None),
            P("leaf", None, "col", None),
            P("leaf", "col", None),
            P("leaf", "col"),
            P("leaf", "col", None),
            P(None, "col", None),
            P(None, None, "col", None),
        ),
        out_specs=(P("leaf", "col", None), P("leaf", "col", None)),
        check_vma=False,
    )
```
